32 devices in a mesh: seq: 16 (over z, y, core), tp: 2 (over x).
Axes of the slice: x: 2, y: 2, z: 4, core: 2. Of those that a mesh axis runs over, the one named last changes fastest.
Arguments:
- queries: bfloat16 [6144, 3072], P('seq', 'tp'), may hold values from -16 to 16
- keys: bfloat16 [6144, 3072], P('seq', 'tp'), may hold values from -6 to 6
- values: bfloat16 [6144, 3072], P('seq', 'tp'), may hold values from -6 to 6
- resid: bfloat16 [6144, 6144], P(('seq', 'tp')), may hold values from -6 to 6
- out_weight: bfloat16 [3072, 6144], P('tp'), may hold values from -0.109375 to 0.109375
- gain: float32 [6144], replicated, may hold values from 0.1 to 1.9
- pair_of_device: int32 [16], replicated, may hold values from 0 to 15, each once
- frame_of_tile: int32 [32], replicated, may hold values from 0 to 8, as said below
Outputs:
- layer_out: bfloat16 [6144, 6144], P(('seq', 'tp'))
The draws below stay inside these ranges and needn't reach their ends.
Inputs may be any that keep to these rules, and one draw needn't show every extreme that they name: `pair_of_device`: each value once. Frames have equal length, 4 tiles; the sequence starts inside frame 0 and ends inside frame 8, so only these two are partial: frame_of_tile[t] = (t + o) // 4 for an offset o from 1 to 3.
All inputs are finite; a program needn't handle non-finite values.
Results may differ from the reference program's by a relative error of at most 0.025.
Values may be sent and summed in bfloat16 or wider, within the bound.
A program may use at most 128 MiB of HBM per device.

```python
import math
import jax
import jax.numpy as jnp
from jax import lax

D = 6144
HEADS = 24
HEAD = 128
FRAMES = 8
SPAN = 192
HD = 3072
NCH = 32
TOKENS = 6144
N_SEQ = 16


def draw_queries(key, part):
    return jnp.clip(jax.random.normal(jax.random.fold_in(key, 11), (TOKENS, HD), jnp.float32), -6.0, 6.0).astype(jnp.bfloat16)


def draw_keys(key, part):
    return jnp.clip(jax.random.normal(jax.random.fold_in(key, 13), (TOKENS, HD), jnp.float32), -6.0, 6.0).astype(jnp.bfloat16)


def draw_frame_of_tile(key, part):
    per_frame = NCH // FRAMES
    offset = jax.random.randint(jax.random.fold_in(key, 4242), (), 1, per_frame, dtype=jnp.int32)
    tile_ids = jnp.arange(NCH, dtype=jnp.int32)
    return ((tile_ids + offset) // per_frame).astype(jnp.int32)


def steps_of(rng, extent, pieces, smallest, high):
    def one(position, blocks):
        steps = jax.random.uniform(jax.random.fold_in(jax.random.fold_in(rng, 6), position), (blocks,), jnp.float32, smallest / len(pieces), high / len(pieces))
        return jnp.repeat(jnp.exp(steps), extent[position] // blocks).reshape((-1,) + (1,) * (len(extent) - position - 1))

    loudness = one(*pieces[0])
    for cut in pieces[1:]:
        loudness = loudness * one(*cut)
    return loudness


def gaussian(rng, dims, deviation, most, pieces=(), kind=jnp.bfloat16):
    drawn = deviation * jax.random.normal(rng, dims, jnp.float32)
    if pieces:
        drawn = drawn * steps_of(rng, dims, pieces, -0.22, 0.18)
    return jnp.clip(drawn, -most, most).astype(kind)


def setup_inputs(seed: int = 0) -> dict:
    streams_of = jax.random.split(jax.random.key(seed), 9)
    return {
        "queries": draw_queries(jax.random.fold_in(streams_of[8], 71), 0),
        "keys": draw_keys(jax.random.fold_in(streams_of[8], 71), 0),
        "values": gaussian(streams_of[2], (TOKENS, HD), 1.0, 6.0, ((0, 16), (1, 2))),
        "resid": gaussian(streams_of[3], (TOKENS, D), 1.0, 6.0, ((0, 32),)),
        "out_weight": gaussian(streams_of[4], (HD, D), HD ** -0.5, 0.109375, ((0, 2),)),
        "gain": jnp.clip(1.0 + 0.18 * jax.random.normal(streams_of[5], (D,), jnp.float32), 0.1, 1.9),
        "pair_of_device": jax.random.permutation(streams_of[6], N_SEQ).astype(jnp.int32),
        "frame_of_tile": draw_frame_of_tile(jax.random.fold_in(streams_of[8], 71), 0),
    }


def slot_frames(pair_of_device, frame_of_tile, tile_count):
    slot_ids = jnp.arange(tile_count, dtype=jnp.int32)
    paired = jnp.repeat(pair_of_device, 2)
    tile_ids = jnp.where(slot_ids % 2 == 0, paired, tile_count - 1 - paired)
    matches = tile_ids[:, None] == jnp.arange(tile_count, dtype=jnp.int32)[None, :]
    return lax.optimization_barrier(jnp.sum(jnp.where(matches, frame_of_tile[None, :], 0), axis=1)).astype(jnp.int32)

def reference(queries, keys, values, resid, out_weight, gain, pair_of_device, frame_of_tile):
    slot_frame = slot_frames(pair_of_device, frame_of_tile, NCH)
    row_frame = jnp.repeat(slot_frame, SPAN)
    key_heads = keys.reshape(TOKENS, HEADS, HEAD).astype(jnp.float32)
    value_heads = values.reshape(TOKENS, HEADS, HEAD).astype(jnp.float32)
    score_scale = 1.0 / math.sqrt(HEAD)

    def one_slot(slot):
        first = (slot * SPAN).astype(jnp.int32)
        query_rows = lax.dynamic_slice_in_dim(queries, first, SPAN, 0)
        query_heads = query_rows.reshape(SPAN, HEADS, HEAD).astype(jnp.float32)
        scores = jnp.einsum('qhd,khd->hqk', query_heads, key_heads) * score_scale
        own_frame = lax.dynamic_slice_in_dim(slot_frame, slot.astype(jnp.int32), 1, 0)
        allowed = (row_frame <= own_frame[0])[None, None, :]
        masked = jnp.where(allowed, scores, jnp.float32(-1e+30))
        row_max = lax.optimization_barrier(jnp.max(masked, axis=-1))
        probs = jnp.where(allowed, jnp.exp(masked - row_max[..., None]), jnp.float32(0.0))
        row_totals = lax.optimization_barrier(jnp.sum(probs, axis=-1))
        probs_bf = probs.astype(jnp.bfloat16).astype(jnp.float32)
        weighted = jnp.einsum('hqk,khd->hqd', probs_bf, value_heads)
        attn = weighted / row_totals[..., None]
        return jnp.transpose(attn, (1, 0, 2)).reshape(SPAN, HD).astype(jnp.bfloat16)
    attn = lax.map(one_slot, jnp.arange(NCH, dtype=jnp.int32)).reshape(TOKENS, HD)
    branch = jnp.dot(attn, out_weight, preferred_element_type=jnp.float32)
    rms = jnp.sqrt(lax.optimization_barrier(jnp.mean(branch * branch, axis=-1)) + 1e-06)
    layer_out = resid.astype(jnp.float32) + gain[None, :] * branch / rms[:, None]
    return layer_out.astype(jnp.bfloat16)
```

```python
import functools
import math

import jax
import jax.numpy as jnp
from jax import lax
from jax.experimental import pallas as pl
from jax.experimental.pallas import tpu as pltpu
from jax.sharding import PartitionSpec as P

HEAD = 128
GROUP = 4


def slot_frames(pair_of_device, frame_of_tile, tile_count):
    slot_ids = jnp.arange(tile_count, dtype=jnp.int32)
    paired = jnp.repeat(pair_of_device, 2)
    tile_ids = jnp.where(slot_ids % 2 == 0, paired, tile_count - 1 - paired)
    matches = tile_ids[:, None] == jnp.arange(tile_count, dtype=jnp.int32)[None, :]
    return jnp.sum(jnp.where(matches, frame_of_tile[None, :], 0), axis=1)


def attend(span, key_tiles, order_ref, seen_ref, q_ref, k_ref, v_ref, o_ref, ks, vs, top, acc):
    tile = pl.program_id(0)
    wide = GROUP * span
    scale = math.log2(math.e) / math.sqrt(HEAD)

    @pl.when(tile == 0)
    def _():
        vs[:, HEAD:] = jnp.ones((key_tiles * span, HEAD), jnp.bfloat16)

        def place(i, carry):
            source = pl.ds(pl.multiple_of(order_ref[i] * span, span), span)
            target = pl.ds(pl.multiple_of(i * span, span), span)
            ks[target, :] = k_ref[source, :]
            vs[target, :HEAD] = v_ref[source, :]
            return carry

        lax.fori_loop(0, key_tiles, place, 0)

    seen = seen_ref[tile]
    q = q_ref[...]
    top[...] = jnp.full(top.shape, -1e30, jnp.float32)
    acc[...] = jnp.zeros(acc.shape, jnp.float32)

    def step(i, masked):
        rows = pl.ds(pl.multiple_of(i * wide, wide), wide)
        scores = lax.dot_general(
            q, ks[rows, :], (((1,), (1,)), ((), ())), preferred_element_type=jnp.float32
        )
        if masked:
            column = lax.broadcasted_iota(jnp.int32, (1, wide), 1)
            scores = jnp.where(column < (seen - i * GROUP) * span, scores, jnp.float32(-1e30))
        old = top[:, :1]
        new = jnp.maximum(old, jnp.max(scores, axis=1, keepdims=True))
        probs = jnp.exp2(scores * scale - new * scale).astype(jnp.bfloat16)
        product = jnp.dot(probs, vs[rows, :], preferred_element_type=jnp.float32)
        acc[...] = acc[...] * jnp.exp2((old - new) * scale) + product
        top[...] = jnp.broadcast_to(new, top.shape)

    full = seen // GROUP

    def body(i, carry):
        step(i, False)
        return carry

    lax.fori_loop(0, full, body, 0)

    @pl.when(full * GROUP < seen)
    def _():
        step(full, True)

    o_ref[...] = (acc[:, :HEAD] / acc[:, HEAD:]).astype(jnp.bfloat16)


def attention(order, seen, q, k, v, span):
    q_tiles = q.shape[0] // span
    key_count = k.shape[0]
    key_tiles = key_count // span
    whole = pl.BlockSpec((key_count, HEAD), lambda i, *_: (0, 0))
    block = pl.BlockSpec((span, HEAD), lambda i, *_: (i, 0))
    return pl.pallas_call(
        functools.partial(attend, span, key_tiles),
        grid_spec=pltpu.PrefetchScalarGridSpec(
            num_scalar_prefetch=2,
            grid=(q_tiles,),
            in_specs=[block, whole, whole],
            out_specs=block,
            scratch_shapes=[
                pltpu.VMEM((key_count, HEAD), jnp.bfloat16),
                pltpu.VMEM((key_count, 2 * HEAD), jnp.bfloat16),
                pltpu.VMEM((span, HEAD), jnp.float32),
                pltpu.VMEM((span, 2 * HEAD), jnp.float32),
            ],
        ),
        out_shape=jax.ShapeDtypeStruct(q.shape, jnp.bfloat16),
        compiler_params=pltpu.CompilerParams(vmem_limit_bytes=40 * 2**20),
        cost_estimate=pl.CostEstimate(
            flops=4 * q.shape[0] * key_count * HEAD,
            bytes_accessed=4 * (q.shape[0] + key_count) * HEAD,
            transcendentals=q.shape[0] * key_count,
        ),
    )(order, seen, q, k, v)


def shifted(x, shift, parts, inner):
    pairs = [
        (a * inner + b, (a + shift) % parts * inner + b) for a in range(parts) for b in range(inner)
    ]
    return lax.ppermute(x, "seq", pairs)


def flipped(x, bit, count):
    return lax.ppermute(x, "seq", [(i, i ^ bit) for i in range(count)])


def local(queries, keys, values, resid, out_weight, gain, pair_of_device, frame_of_tile):
    rows, width = queries.shape
    heads = width // HEAD
    span = rows // 2
    seq_count = lax.axis_size("seq")
    tp_count = lax.axis_size("tp")
    model = out_weight.shape[1]
    parts = math.gcd(heads, seq_count)
    inner = seq_count // parts
    steps = heads // parts
    me = lax.axis_index("seq")
    part = me // inner
    place = me % inner

    frames = slot_frames(pair_of_device, frame_of_tile, 2 * seq_count).reshape(seq_count, 2)
    sources = (part - jnp.arange(parts, dtype=jnp.int32)) % parts
    flips = [0]
    bits = [inner >> (n + 1) for n in range(inner.bit_length() - 1)]
    for bit in bits:
        flips = flips + [f ^ bit for f in flips]
    places = place ^ jnp.array(flips, jnp.int32)
    key_frames = frames[sources[None, :] * inner + places[:, None]].reshape(-1)
    query_frames = frames[sources * inner + place].reshape(-1)
    order = jnp.argsort(key_frames).astype(jnp.int32)
    seen = jnp.sum(key_frames[None, :] <= query_frames[:, None], axis=1).astype(jnp.int32)

    weight = out_weight.reshape(parts, steps, HEAD, model)
    by_step = weight.transpose(1, 0, 2, 3).reshape(steps, parts * HEAD, model)
    split = tp_count == 2 and inner % 2 == 0
    early = steps - 1 if split else steps
    if split:
        half = parts * HEAD // 2
        mine = lax.dynamic_slice_in_dim(by_step[early], (place % 2) * half, half, 0)
        first = lax.ppermute(mine, "tp", [(0, 1), (1, 0)])
        second = flipped(first, 1, seq_count)
        low = place % 2 == 0
        peer_weight = jnp.concatenate([jnp.where(low, first, second), jnp.where(low, second, first)], axis=0)

    packed = jnp.stack(
        [x.reshape(rows, parts, steps, HEAD).transpose(2, 1, 0, 3) for x in (keys, values, queries)], axis=2
    )

    attn = []
    for j in range(steps):
        blocks = packed[j]

        def pick(shift, blocks=blocks):
            return lax.dynamic_index_in_dim(blocks, (part + shift) % parts, 0, keepdims=False)

        got = [pick(0)] + [shifted(pick(s), s, parts, inner) for s in range(1, parts)]
        q = jnp.concatenate([g[2] for g in got], axis=0)
        kv = jnp.stack([g[:2] for g in got], axis=1).reshape(2, parts * rows, HEAD)
        for bit in bits:
            kv = jnp.concatenate([kv, flipped(kv, bit, seq_count)], axis=1)
        out = attention(order, seen, q, kv[0], kv[1], span).reshape(parts, rows, HEAD)
        back = [out[0]] + [shifted(out[s], parts - s, parts, inner) for s in range(1, parts)]
        ring = jnp.stack(back + back, axis=0)
        turned = lax.dynamic_slice_in_dim(ring, (parts - part) % parts, parts, 0)
        attn.append(turned.transpose(1, 0, 2).reshape(rows, parts * HEAD))

    if split:
        t = lax.axis_index("tp")
        front = jnp.concatenate(attn[:early], axis=1)
        front_weight = by_step[:early].reshape(early * parts * HEAD, model)
        theirs = lax.dynamic_slice_in_dim(front, (1 - t) * span, span, 0)
        ours = lax.dynamic_slice_in_dim(front, t * span, span, 0)
        sent = jnp.dot(theirs, front_weight, preferred_element_type=jnp.float32).astype(jnp.bfloat16)
        come = lax.ppermute(sent, "tp", [(0, 1), (1, 0)])
        last_theirs = lax.dynamic_slice_in_dim(attn[-1], (1 - t) * span, span, 0)
        last_ours = lax.dynamic_slice_in_dim(attn[-1], t * span, span, 0)
        last_come = lax.ppermute(last_theirs, "tp", [(0, 1), (1, 0)])
        branch = (
            jnp.dot(ours, front_weight, preferred_element_type=jnp.float32)
            + jnp.dot(last_ours, by_step[early], preferred_element_type=jnp.float32)
            + jnp.dot(last_come, peer_weight, preferred_element_type=jnp.float32)
            + come.astype(jnp.float32)
        )
    else:
        full = jnp.concatenate(attn, axis=1)
        product = jnp.dot(full, by_step.reshape(width, model), preferred_element_type=jnp.float32)
        branch = lax.psum_scatter(
            product.astype(jnp.bfloat16), "tp", scatter_dimension=0, tiled=True
        ).astype(jnp.float32)
    rms = jnp.sqrt(jnp.mean(branch * branch, axis=-1) + 1e-06)
    layer_out = resid.astype(jnp.float32) + gain[None, :] * branch / rms[:, None]
    return layer_out.astype(jnp.bfloat16)


def solution(mesh):
    in_specs = (
        P("seq", "tp"),
        P("seq", "tp"),
        P("seq", "tp"),
        P(("seq", "tp"), None),
        P("tp", None),
        P(),
        P(),
        P(),
    )
    out_specs = P(("seq", "tp"), None)
    return jax.shard_map(local, mesh=mesh, in_specs=in_specs, out_specs=out_specs, check_vma=False)
```

```python
import functools
import math

import jax
import jax.numpy as jnp
from jax import lax
from jax.experimental import pallas as pl
from jax.experimental.pallas import tpu as pltpu
from jax.sharding import PartitionSpec as P

HEAD = 128
GROUP = 4


def slot_frames(pair_of_device, frame_of_tile, tile_count):
    slot_ids = jnp.arange(tile_count, dtype=jnp.int32)
    paired = jnp.repeat(pair_of_device, 2)
    tile_ids = jnp.where(slot_ids % 2 == 0, paired, tile_count - 1 - paired)
    matches = tile_ids[:, None] == jnp.arange(tile_count, dtype=jnp.int32)[None, :]
    return jnp.sum(jnp.where(matches, frame_of_tile[None, :], 0), axis=1)


def attend(span, key_tiles, order_ref, seen_ref, q_ref, k_ref, v_ref, o_ref, ks, vs, kept, top, acc):
    tile = pl.program_id(0)
    wide = GROUP * span
    blocks = wide // HEAD
    scale = math.log2(math.e) / math.sqrt(HEAD)

    @pl.when(tile == 0)
    def _():
        vs[:, HEAD:] = jnp.ones((key_tiles * span, HEAD), jnp.bfloat16)

        def place(i, carry):
            source = pl.ds(pl.multiple_of(order_ref[i] * span, span), span)
            target = pl.ds(pl.multiple_of(i * span, span), span)
            ks[target, :] = k_ref[source, :]
            vs[target, :HEAD] = v_ref[source, :]
            return carry

        lax.fori_loop(0, key_tiles, place, 0)

    seen = seen_ref[tile]
    top[...] = jnp.full(top.shape, -1e30, jnp.float32)
    acc[...] = jnp.zeros(acc.shape, jnp.float32)

    def score(i, count, masked):
        best = top[...]
        for n in range(count):
            rows = pl.ds(pl.multiple_of((i + n) * wide, wide), wide)
            scores = lax.dot_general(
                q_ref[...], ks[rows, :], (((1,), (1,)), ((), ())), preferred_element_type=jnp.float32
            )
            if masked:
                column = lax.broadcasted_iota(jnp.int32, (1, wide), 1)
                scores = jnp.where(column < (seen - i * GROUP) * span, scores, jnp.float32(-1e30))
            kept[i + n] = scores
            for c in range(blocks):
                best = jnp.maximum(best, scores[:, c * HEAD : (c + 1) * HEAD])
        top[...] = best

    def weigh(i, count):
        peak = jnp.concatenate([top[...]] * blocks, axis=1)
        total = acc[...]
        for n in range(count):
            rows = pl.ds(pl.multiple_of((i + n) * wide, wide), wide)
            probs = jnp.exp2(kept[i + n] * scale - peak).astype(jnp.bfloat16)
            total = total + jnp.dot(probs, vs[rows, :], preferred_element_type=jnp.float32)
        acc[...] = total

    full = seen // GROUP
    used = (seen + GROUP - 1) // GROUP

    def score_pair(i, carry):
        score(2 * i, 2, False)
        return carry

    def weigh_pair(i, carry):
        weigh(2 * i, 2)
        return carry

    lax.fori_loop(0, full // 2, score_pair, 0)

    @pl.when(full % 2 == 1)
    def _():
        score(full - 1, 1, False)

    @pl.when(full < used)
    def _():
        score(full, 1, True)

    top[...] = jnp.broadcast_to(jnp.max(top[...], axis=1, keepdims=True) * scale, top.shape)
    lax.fori_loop(0, used // 2, weigh_pair, 0)

    @pl.when(used % 2 == 1)
    def _():
        weigh(used - 1, 1)

    o_ref[...] = (acc[:, :HEAD] / acc[:, HEAD:]).astype(jnp.bfloat16)


def attention(order, seen, q, k, v, span):
    q_tiles = q.shape[0] // span
    key_count = k.shape[0]
    key_tiles = key_count // span
    whole = pl.BlockSpec((key_count, HEAD), lambda i, *_: (0, 0))
    block = pl.BlockSpec((span, HEAD), lambda i, *_: (i, 0))
    return pl.pallas_call(
        functools.partial(attend, span, key_tiles),
        grid_spec=pltpu.PrefetchScalarGridSpec(
            num_scalar_prefetch=2,
            grid=(q_tiles,),
            in_specs=[block, whole, whole],
            out_specs=block,
            scratch_shapes=[
                pltpu.VMEM((key_count, HEAD), jnp.bfloat16),
                pltpu.VMEM((key_count, 2 * HEAD), jnp.bfloat16),
                pltpu.VMEM((key_tiles // GROUP, span, GROUP * span), jnp.float32),
                pltpu.VMEM((span, HEAD), jnp.float32),
                pltpu.VMEM((span, 2 * HEAD), jnp.float32),
            ],
        ),
        out_shape=jax.ShapeDtypeStruct(q.shape, jnp.bfloat16),
        compiler_params=pltpu.CompilerParams(vmem_limit_bytes=40 * 2**20),
        cost_estimate=pl.CostEstimate(
            flops=4 * q.shape[0] * key_count * HEAD,
            bytes_accessed=4 * (q.shape[0] + key_count) * HEAD,
            transcendentals=q.shape[0] * key_count,
        ),
    )(order, seen, q, k, v)


def shifted(x, shift, parts, inner):
    pairs = [
        (a * inner + b, (a + shift) % parts * inner + b) for a in range(parts) for b in range(inner)
    ]
    return lax.ppermute(x, "seq", pairs)


def flipped(x, bit, count):
    return lax.ppermute(x, "seq", [(i, i ^ bit) for i in range(count)])


def local(queries, keys, values, resid, out_weight, gain, pair_of_device, frame_of_tile):
    rows, width = queries.shape
    heads = width // HEAD
    span = rows // 2
    seq_count = lax.axis_size("seq")
    tp_count = lax.axis_size("tp")
    model = out_weight.shape[1]
    parts = math.gcd(heads, seq_count)
    inner = seq_count // parts
    steps = heads // parts
    me = lax.axis_index("seq")
    part = me // inner
    place = me % inner

    frames = slot_frames(pair_of_device, frame_of_tile, 2 * seq_count).reshape(seq_count, 2)
    sources = (part - jnp.arange(parts, dtype=jnp.int32)) % parts
    flips = [0]
    bits = [inner >> (n + 1) for n in range(inner.bit_length() - 1)]
    for bit in bits:
        flips = flips + [f ^ bit for f in flips]
    places = place ^ jnp.array(flips, jnp.int32)
    key_frames = frames[sources[None, :] * inner + places[:, None]].reshape(-1)
    query_frames = frames[sources * inner + place].reshape(-1)
    order = jnp.argsort(key_frames).astype(jnp.int32)
    seen = jnp.sum(key_frames[None, :] <= query_frames[:, None], axis=1).astype(jnp.int32)

    deep = parts * HEAD
    split = tp_count == 2 and inner % 2 == 0
    early = steps - 1 if split else steps
    if split:
        half = deep // 2
        mine = lax.dynamic_slice_in_dim(out_weight, early * deep + (place % 2) * half, half, 0)
        first = lax.ppermute(mine, "tp", [(0, 1), (1, 0)])
        second = flipped(first, 1, seq_count)
        low = place % 2 == 0
        peer_weight = jnp.concatenate([jnp.where(low, first, second), jnp.where(low, second, first)], axis=0)

    packed = jnp.stack(
        [x.reshape(rows, steps, parts, HEAD).transpose(1, 2, 0, 3) for x in (keys, values, queries)], axis=2
    )

    def tied(x, other):
        return lax.optimization_barrier((x, other))[0]

    got = []
    for j in range(steps):
        blocks = packed[j]

        def pick(shift, blocks=blocks):
            return lax.dynamic_index_in_dim(blocks, (part + shift) % parts, 0, keepdims=False)

        got.append([pick(0)] + [shifted(pick(s), s, parts, inner) for s in range(1, parts)])

    if split:
        t = lax.axis_index("tp")
    attn, outs = [], []
    for j in range(steps):
        q = jnp.concatenate([g[2] for g in got[j]], axis=0)
        kv = jnp.stack([g[:2] for g in got[j]], axis=1).reshape(2, parts * rows, HEAD)
        if j >= 2:
            kv = tied(kv, outs[j - 2])
        for bit in bits:
            if bit == bits[-1] and j >= 1:
                kv = tied(kv, outs[j - 1])
            kv = jnp.concatenate([kv, flipped(kv, bit, seq_count)], axis=1)
        if split and j == early:
            front = jnp.concatenate(attn, axis=1)
            front_weight = out_weight[: early * deep]
            theirs = lax.dynamic_slice_in_dim(front, (1 - t) * span, span, 0)
            ours = lax.dynamic_slice_in_dim(front, t * span, span, 0)
            sent = jnp.dot(theirs, front_weight, preferred_element_type=jnp.float32).astype(jnp.bfloat16)
            come = lax.ppermute(sent, "tp", [(0, 1), (1, 0)])
            q = tied(q, sent)
        out = attention(order, seen, q, kv[0], kv[1], span)
        outs.append(out)
        out = out.reshape(parts, rows, HEAD)
        back = [out[0]] + [shifted(out[s], parts - s, parts, inner) for s in range(1, parts)]
        ring = jnp.stack(back + back, axis=0)
        turned = lax.dynamic_slice_in_dim(ring, (parts - part) % parts, parts, 0)
        attn.append(turned.transpose(1, 0, 2).reshape(rows, deep))

    if split:
        last_theirs = lax.dynamic_slice_in_dim(attn[-1], (1 - t) * span, span, 0)
        last_ours = lax.dynamic_slice_in_dim(attn[-1], t * span, span, 0)
        last_come = lax.ppermute(last_theirs, "tp", [(0, 1), (1, 0)])
        branch = (
            jnp.dot(ours, front_weight, preferred_element_type=jnp.float32)
            + jnp.dot(last_ours, out_weight[early * deep :], preferred_element_type=jnp.float32)
            + jnp.dot(last_come, peer_weight, preferred_element_type=jnp.float32)
            + come.astype(jnp.float32)
        )
    else:
        full = jnp.concatenate(attn, axis=1)
        product = jnp.dot(full, out_weight, preferred_element_type=jnp.float32)
        branch = lax.psum_scatter(
            product.astype(jnp.bfloat16), "tp", scatter_dimension=0, tiled=True
        ).astype(jnp.float32)
    rms = jnp.sqrt(jnp.mean(branch * branch, axis=-1) + 1e-06)
    layer_out = resid.astype(jnp.float32) + gain[None, :] * branch / rms[:, None]
    return layer_out.astype(jnp.bfloat16)


def solution(mesh):
    in_specs = (
        P("seq", "tp"),
        P("seq", "tp"),
        P("seq", "tp"),
        P(("seq", "tp"), None),
        P("tp", None),
        P(),
        P(),
        P(),
    )
    out_specs = P(("seq", "tp"), None)
    return jax.shard_map(local, mesh=mesh, in_specs=in_specs, out_specs=out_specs, check_vma=False)
```
